32 devices in a mesh: groups: 2 (over y), atoms: 4 (over z), kvec: 2 (over x), rep: 2 (over core).
Axes of the slice: x: 2, y: 2, z: 4, core: 2. Of those that a mesh axis runs over, the one named last changes fastest.
Arguments:
- positions: float32 [4, 3, 8192], P(('groups', 'rep'), None, 'atoms'), parts along dimension 0, may hold values from 0 to 1
- features: bfloat16 [4, 8192, 256], P(('groups', 'rep'), 'atoms'), parts along dimension 0
- species: int32 [4, 8192], P(('groups', 'rep'), 'atoms'), parts along dimension 0, may hold values from 0 to 7
- cell_length: float32 [4], P(('groups', 'rep')), parts along dimension 0, may hold values from 40 to 60
- energy_ref: float32 [4], P(('groups', 'rep')), parts along dimension 0, may hold values from -12 to -6
- miller_index: int32 [3, 2048], P(None, 'kvec'), may hold values from -8 to 8, as said below
- weight_in: bfloat16 [256, 512], replicated, may hold values from -0.375 to 0.375
- weight_mid: bfloat16 [512, 512], replicated, may hold values from -0.25 to 0.25
- weight_out: bfloat16 [512, 32], replicated, may hold values from -0.25 to 0.25
- species_bias: float32 [8, 512], replicated, may hold values from -3 to 3
Outputs:
- potential: float32 [4, 8192, 32], P(('groups', 'rep'), ('atoms', 'kvec')), parts along dimension 0
- energy: float32 [4], P(('groups', 'rep')), parts along dimension 0
- grad_in: float32 [512, 512], P('groups'), parts along dimension 0
- grad_mid: float32 [1024, 512], P('groups'), parts along dimension 0
- grad_out: float32 [1024, 32], P('groups'), parts along dimension 0
- grad_bias: float32 [16, 512], P('groups'), parts along dimension 0
The draws below stay inside these ranges and needn't reach their ends.
There are 2 independent parts, one for each index of `groups`. The reference program is written for one: setup_inputs(seed, part) draws one part's arguments, and reference() takes and returns one part's arrays. A program takes and returns all parts, laid end to end along the dimension named above; an argument that names none is the same for every part. Nothing has to cross between parts.
Inputs may be any that keep to these rules, and one draw needn't show every extreme that they name: No column of miller_index is all zeros.
All inputs are finite; a program needn't handle non-finite values.
Results may differ from the reference program's by a relative error of at most 0.0046.
Values may be sent and summed in bfloat16 or wider, within the bound.
A program may use at most 64 MiB of HBM per device.

```python
import math
import jax
import jax.numpy as jnp
from jax import lax

KVECS = 2048
C = 32
IN = 256
HID = 512
SPECIES = 8
MMAX = 8
CELLS = 2
ATOMS = 8192


def draw_positions(key, part):
    site_key, jitter_key, loose_key, pick_key = jax.random.split(key, 4)
    share = min(1.0, 24.0 / math.sqrt(ATOMS))
    spread = 0.02
    lattice_sites = jax.random.randint(site_key, (CELLS, 3, ATOMS), 0, 4, dtype=jnp.int32).astype(jnp.float32) * 0.25
    jitter = jax.random.uniform(jitter_key, (CELLS, 3, ATOMS), jnp.float32, 0.0, spread)
    ordered = lattice_sites + jitter
    loose = jax.random.uniform(loose_key, (CELLS, 3, ATOMS), jnp.float32, 0.0, 1.0)
    chosen = jax.random.uniform(pick_key, (CELLS, 1, ATOMS), jnp.float32, 0.0, 1.0) < share
    return jnp.where(chosen, ordered, loose).astype(jnp.float32)


def draw_features(key, part):
    base_key = jax.random.fold_in(key, 0)
    atom_order = jnp.arange(ATOMS, dtype=jnp.float32)
    row_scale = 1.0 + 2.0 * atom_order / (ATOMS - 1)
    samples = jax.random.normal(base_key, (CELLS, ATOMS, IN), jnp.float32)
    return (samples * row_scale[None, :, None]).astype(jnp.bfloat16)


def draw_miller_index(key, part):
    drawn_index = jax.random.randint(key, (3, KVECS), -MMAX, MMAX + 1, dtype=jnp.int32)
    all_zero = (drawn_index[0] == 0) & (drawn_index[1] == 0) & (drawn_index[2] == 0)
    first_row = jnp.where(all_zero, 1, drawn_index[0])
    return jnp.stack([first_row, drawn_index[1], drawn_index[2]]).astype(jnp.int32)


def place_ends(result, key, least, top_value):
    longest = result.shape.index(max(result.shape))
    spots = []
    for shift in (0, 1):
        where = [jax.random.randint(jax.random.fold_in(key, axis), (), 0, length) for axis, length in enumerate(result.shape)]
        where[longest] = (where[longest] + shift) % result.shape[longest]
        spots.append(tuple(where))
    return result.at[spots[0]].set(least).at[spots[1]].set(top_value)


def shard_levels(rng, shape, shards, low, top_value):
    def one(axis_at, shards_of):
        steps = jax.random.uniform(jax.random.fold_in(jax.random.fold_in(rng, 6), axis_at), (shards_of,), jnp.float32, low / len(shards), top_value / len(shards))
        return jnp.repeat(jnp.exp(steps), shape[axis_at] // shards_of).reshape((-1,) + (1,) * (len(shape) - axis_at - 1))

    factor_of = one(*shards[0])
    for cut in shards[1:]:
        factor_of = factor_of * one(*cut)
    return factor_of


def bell_draw(stream_key, shape, scale, reach, held_as=jnp.bfloat16):
    return jnp.clip(scale * jax.random.normal(stream_key, shape, jnp.float32), -reach, reach).astype(held_as)


def setup_inputs(seed: int = 0, part: int = 0) -> dict:
    key_list = jax.random.split(jax.random.key(seed), 11)
    part_splits = jax.random.split(jax.random.fold_in(key_list[10], part), 11)
    return {
        "positions": draw_positions(jax.random.fold_in(jax.random.fold_in(key_list[10], part), 71), part),
        "features": draw_features(jax.random.fold_in(jax.random.fold_in(key_list[10], part), 71), part),
        "species": place_ends(jax.random.randint(part_splits[2], (CELLS, ATOMS), 0, SPECIES), jax.random.fold_in(part_splits[2], 1), 0, SPECIES - 1).astype(jnp.int32),
        "cell_length": jnp.clip(40.0 + 20.0 * jax.random.uniform(part_splits[3], (CELLS,), jnp.float32) ** shard_levels(part_splits[3], (CELLS,), ((0, 2),), -0.2, 0.2), 40.0, 60.0),
        "energy_ref": jnp.clip(-12.0 + 6.0 * jax.random.uniform(part_splits[4], (CELLS,), jnp.float32) ** shard_levels(part_splits[4], (CELLS,), ((0, 2),), -0.2, 0.2), -12.0, -6.0),
        "miller_index": draw_miller_index(jax.random.fold_in(key_list[10], 71), part),
        "weight_in": bell_draw(key_list[6], (IN, HID), IN ** -0.5, 0.375),
        "weight_mid": bell_draw(key_list[7], (HID, HID), HID ** -0.5, 0.25),
        "weight_out": bell_draw(key_list[8], (HID, C), HID ** -0.5, 0.25),
        "species_bias": bell_draw(key_list[9], (SPECIES, HID), 0.5, 3.0, jnp.float32),
    }


TWO_PI = 2.0 * math.pi
HIGHEST = lax.Precision.HIGHEST

def phase_tiles(coord_rows, miller_float):
    phase_turns = coord_rows[0][:, None] * miller_float[0][None, :] + coord_rows[1][:, None] * miller_float[1][None, :] + coord_rows[2][:, None] * miller_float[2][None, :]
    phase_angle = TWO_PI * phase_turns
    return jnp.concatenate([jnp.cos(phase_angle), jnp.sin(phase_angle)], axis=1).astype(jnp.bfloat16)

def wave_weights(miller_float, cell_size, atoms_total):
    index_square = miller_float[0] * miller_float[0] + miller_float[1] * miller_float[1] + miller_float[2] * miller_float[2]
    factor = TWO_PI / cell_size
    wave_square = index_square * (factor * factor)
    decay_base = jnp.exp(-0.5 * wave_square) / wave_square * (1.0 / math.sqrt(atoms_total * KVECS))
    return jnp.concatenate([decay_base, decay_base])

def contract_rows(left_rows, right_rows):
    return lax.dot_general(left_rows, right_rows, (((0,), (0,)), ((), ())), preferred_element_type=jnp.float32)

def silu_slope(linear):
    sigmoid_value = jax.nn.sigmoid(linear)
    return sigmoid_value * (1.0 + linear * (1.0 - sigmoid_value))

def forward(atom_features, atom_species, weight_in, weight_mid, weight_out, species_bias):
    kinds = jnp.arange(species_bias.shape[0], dtype=jnp.int32)
    onehot = (atom_species[:, None] == kinds[None, :]).astype(jnp.float32)
    bias_rows = jnp.dot(onehot, species_bias, precision=HIGHEST, preferred_element_type=jnp.float32)
    linear_one = jnp.dot(atom_features, weight_in, preferred_element_type=jnp.float32) + bias_rows
    hidden_one = jax.nn.silu(linear_one).astype(jnp.bfloat16)
    linear_two = jnp.dot(hidden_one, weight_mid, preferred_element_type=jnp.float32)
    hidden_two = jax.nn.silu(linear_two).astype(jnp.bfloat16)
    charges = jnp.dot(hidden_two, weight_out, preferred_element_type=jnp.float32).astype(jnp.bfloat16)
    return (onehot, linear_one, hidden_one, linear_two, hidden_two, charges)

def backward(atom_features, onehot, linear_one, hidden_one, linear_two, hidden_two, grad_charges, weight_mid, weight_out):
    grad_out = contract_rows(hidden_two, grad_charges)
    back_two = lax.dot_general(grad_charges, weight_out, (((1,), (1,)), ((), ())), preferred_element_type=jnp.float32)
    grad_two = (back_two * silu_slope(linear_two)).astype(jnp.bfloat16)
    grad_mid = contract_rows(hidden_one, grad_two)
    back_one = lax.dot_general(grad_two, weight_mid, (((1,), (1,)), ((), ())), preferred_element_type=jnp.float32)
    grad_one = (back_one * silu_slope(linear_one)).astype(jnp.bfloat16)
    grad_in = contract_rows(atom_features, grad_one)
    grad_bias = contract_rows(onehot.astype(jnp.bfloat16), grad_one)
    return (grad_in, grad_mid, grad_out, grad_bias)

def reference(positions, features, species, cell_length, energy_ref, miller_index, weight_in, weight_mid, weight_out, species_bias):
    miller_float = miller_index.astype(jnp.float32)
    step_rows = math.gcd(ATOMS, 2048)
    blocks = ATOMS // step_rows
    potentials = []
    energies = []
    summed = None
    for cell_index in range(CELLS):
        column_weights = wave_weights(miller_float, cell_length[cell_index], ATOMS)
        onehot, linear_one, hidden_one, linear_two, hidden_two, charges = forward(features[cell_index], species[cell_index], weight_in, weight_mid, weight_out, species_bias)
        coord_blocks = jnp.transpose(positions[cell_index].reshape(3, blocks, step_rows), (1, 0, 2))
        charge_blocks = charges.reshape(blocks, step_rows, C)

        def add_block(running, block_data):
            coord_rows, charge_rows = block_data
            return (running + contract_rows(charge_rows, phase_tiles(coord_rows, miller_float)), None)
        panels, _ = lax.scan(add_block, jnp.zeros((C, 2 * KVECS), jnp.float32), (coord_blocks, charge_blocks))
        energy = jnp.sum(panels * panels * column_weights[None, :]) / ATOMS
        weighted = (panels * column_weights[None, :]).astype(jnp.bfloat16)

        def potential_block(coord_rows):
            return lax.dot_general(phase_tiles(coord_rows, miller_float), weighted, (((1,), (1,)), ((), ())), preferred_element_type=jnp.float32)
        potential = lax.map(potential_block, coord_blocks).reshape(ATOMS, C)
        loss_scale = (energy - energy_ref[cell_index]) * (2.0 / ATOMS)
        grad_charges = (loss_scale * potential).astype(jnp.bfloat16)
        gradients = backward(features[cell_index], onehot, linear_one, hidden_one, linear_two, hidden_two, grad_charges, weight_mid, weight_out)
        if summed is None:
            summed = gradients
        else:
            summed = tuple((first_sum + second_sum for first_sum, second_sum in zip(summed, gradients)))
        potentials.append(potential)
        energies.append(energy)
    return (jnp.stack(potentials), jnp.stack(energies), summed[0], summed[1], summed[2], summed[3])
```

```python
import functools
import math

import jax
import jax.numpy as jnp
from jax import lax
from jax.experimental import pallas as pl
from jax.experimental.pallas import tpu as pltpu
from jax.sharding import PartitionSpec as P

KVECS = 2048


TWO_PI = 2.0 * math.pi
HIGHEST = lax.Precision.HIGHEST


def phase_tiles(coord_rows, miller_float):
    phase_turns = (
        coord_rows[0][:, None] * miller_float[0][None, :]
        + coord_rows[1][:, None] * miller_float[1][None, :]
        + coord_rows[2][:, None] * miller_float[2][None, :]
    )
    phase_angle = TWO_PI * phase_turns
    return jnp.concatenate([jnp.cos(phase_angle), jnp.sin(phase_angle)], axis=1).astype(
        jnp.bfloat16
    )


def wave_weights(miller_float, cell_size, atoms_total):
    index_square = (
        miller_float[0] * miller_float[0]
        + miller_float[1] * miller_float[1]
        + miller_float[2] * miller_float[2]
    )
    factor = TWO_PI / cell_size
    wave_square = index_square * (factor * factor)
    decay_base = jnp.exp(-0.5 * wave_square) / wave_square * (1.0 / math.sqrt(atoms_total * KVECS))
    return jnp.concatenate([decay_base, decay_base])


def contract_rows(left_rows, right_rows):
    return lax.dot_general(
        left_rows, right_rows, (((0,), (0,)), ((), ())), preferred_element_type=jnp.float32
    )


def silu_slope(linear):
    sigmoid_value = jax.nn.sigmoid(linear)
    return sigmoid_value * (1.0 + linear * (1.0 - sigmoid_value))


def forward(atom_features, atom_species, weight_in, weight_mid, weight_out, species_bias):
    kinds = jnp.arange(species_bias.shape[0], dtype=jnp.int32)
    onehot = (atom_species[:, None] == kinds[None, :]).astype(jnp.float32)
    bias_rows = jnp.dot(onehot, species_bias, precision=HIGHEST, preferred_element_type=jnp.float32)
    linear_one = jnp.dot(atom_features, weight_in, preferred_element_type=jnp.float32) + bias_rows
    hidden_one = jax.nn.silu(linear_one).astype(jnp.bfloat16)
    linear_two = jnp.dot(hidden_one, weight_mid, preferred_element_type=jnp.float32)
    hidden_two = jax.nn.silu(linear_two).astype(jnp.bfloat16)
    charges = jnp.dot(hidden_two, weight_out, preferred_element_type=jnp.float32).astype(
        jnp.bfloat16
    )
    return (onehot, linear_one, hidden_one, linear_two, hidden_two, charges)


def backward(
    atom_features,
    onehot,
    linear_one,
    hidden_one,
    linear_two,
    hidden_two,
    grad_charges,
    weight_mid,
    weight_out,
):
    grad_out = contract_rows(hidden_two, grad_charges)
    back_two = lax.dot_general(
        grad_charges, weight_out, (((1,), (1,)), ((), ())), preferred_element_type=jnp.float32
    )
    grad_two = (back_two * silu_slope(linear_two)).astype(jnp.bfloat16)
    grad_mid = contract_rows(hidden_one, grad_two)
    back_one = lax.dot_general(
        grad_two, weight_mid, (((1,), (1,)), ((), ())), preferred_element_type=jnp.float32
    )
    grad_one = (back_one * silu_slope(linear_one)).astype(jnp.bfloat16)
    grad_in = contract_rows(atom_features, grad_one)
    grad_bias = contract_rows(onehot.astype(jnp.bfloat16), grad_one)
    return (grad_in, grad_mid, grad_out, grad_bias)


def plain_body(
    positions,
    features,
    species,
    cell_length,
    energy_ref,
    miller_index,
    weight_in,
    weight_mid,
    weight_out,
    species_bias,
):
    block_rows = positions.shape[2]
    kvec_count = miller_index.shape[1]
    channels = weight_out.shape[1]
    atoms_total = block_rows * lax.axis_size("atoms")
    quarter = block_rows // lax.axis_size("kvec")
    own_first = lax.axis_index("kvec") * quarter
    miller_float = miller_index.astype(jnp.float32)
    column_weights = wave_weights(miller_float, cell_length[0], atoms_total)
    coords = positions[0]
    step_rows = math.gcd(block_rows, 512)
    stored = jnp.concatenate(
        [
            phase_tiles(lax.slice_in_dim(coords, offset, offset + step_rows, axis=1), miller_float)
            for offset in range(0, block_rows, step_rows)
        ],
        axis=0,
    )

    def tile_rows(first_row, row_count):
        return lax.dynamic_slice_in_dim(stored, first_row, row_count, 0)

    zero_panels = jnp.zeros((channels, 2 * kvec_count), jnp.float32)
    own_features = features[0]
    own_species = species[0]
    onehot, linear_one, hidden_one, linear_two, hidden_two, charges = forward(
        own_features, own_species, weight_in, weight_mid, weight_out, species_bias
    )
    running = zero_panels
    row_count = charges.shape[0]
    piece_rows = math.gcd(row_count, 512)
    for inner_start in range(0, row_count, piece_rows):
        phase_rows = tile_rows(0 + inner_start, piece_rows)
        running = running + contract_rows(
            lax.slice_in_dim(charges, inner_start, inner_start + piece_rows, axis=0), phase_rows
        )
    summed = lax.psum(running, "atoms")
    energy_sum = lax.psum(jnp.sum(summed * summed * column_weights[None, :]).reshape(1), "kvec")
    weighted = (summed * column_weights[None, :]).astype(jnp.bfloat16)
    energy = energy_sum / atoms_total
    piece_rows = math.gcd(block_rows, 512)
    pieces = []
    for inner_start in range(0, block_rows, piece_rows):
        phase_rows = tile_rows(0 + inner_start, piece_rows)
        pieces.append(
            lax.dot_general(
                phase_rows, weighted, (((1,), (1,)), ((), ())), preferred_element_type=jnp.float32
            )
        )
    used_potential = lax.psum(jnp.concatenate(pieces, axis=0), "kvec")
    own_potential = lax.dynamic_slice_in_dim(used_potential, own_first, quarter, 0)
    loss_scale = (energy[0] - energy_ref[0]) * (2.0 / atoms_total)
    grad_charges = (loss_scale * used_potential).astype(jnp.bfloat16)
    local_in, local_mid, local_out, local_bias = backward(
        own_features,
        onehot,
        linear_one,
        hidden_one,
        linear_two,
        hidden_two,
        grad_charges,
        weight_mid,
        weight_out,
    )
    grad_in, grad_mid, grad_out, grad_bias = lax.psum(
        (local_in, local_mid, local_out, local_bias), ("atoms", "rep")
    )
    return (own_potential[None], energy, grad_in, grad_mid, grad_out, grad_bias)


TURN_SHIFT = 1.5 * 2.0**23
SINE = (4.442867834, -7.307441175, 3.594769894, -0.784331973)
COSINE = (1.414213496, -6.978850946, 5.739460314, -1.883557438, 0.310686957)
ROWS = 256
STRIP = 16
BF = jnp.bfloat16
F32 = jnp.float32


def mul(left, right, dims):
    return lax.dot_general(left, right, ((dims[:1], dims[1:]), ((), ())), preferred_element_type=F32)


def split_three(value):
    high = value.astype(BF).astype(F32)
    rest = value - high
    middle = rest.astype(BF).astype(F32)
    return high, middle, rest - middle


def fused(
    nz, rows_b,
    pos, feat, spec, clen, eref, mill, w_in, w_mid, w_out, bias,
    pot_o, en_o, gin_o, gmid_o, gout_o, gbias_o,
    pos_f, pos_s, mill_f, mill_s, bias_f, bias_s, hot, out_t, cw,
    h1, h2, slope1, slope2, ch, turns, phases, panels,
    pz_s, pz_r, w_all, en_mine, en_z, en_x, en_sum,
    pot, pot_s, pot_r, gc, g2, g1,
    ga, ra_s, ra_r, xa_s, xa_r, za_s, za_r, all_a,
    gb, rb_s, rb_r, xb_s, xb_r, zb_s, zb_r, all_b,
    send, recv,
):
    z = lax.axis_index("atoms")
    x = lax.axis_index("kvec")
    r = lax.axis_index("rep")
    atoms = pos.shape[2]
    half = atoms // 2
    kv = mill.shape[1]
    channels = w_out.shape[1]
    width = 2 * kv // nz
    atoms_total = atoms * nz
    to_x = {"kvec": 1 - x}
    to_r = {"rep": 1 - r}

    def to_z(step):
        return {"atoms": lax.rem(z + step, nz)}

    barrier = pltpu.get_barrier_semaphore()
    peers = [to_x, to_r] + [to_z(step) for step in range(1, nz)]
    for peer in peers:
        pl.semaphore_signal(barrier, inc=1, device_id=peer, device_id_type=pl.DeviceIdType.MESH)

    count = [0]

    def copy(src, dst, peer):
        slot = count[0]
        count[0] += 1
        made = pltpu.make_async_remote_copy(
            src_ref=src, dst_ref=dst, send_sem=send.at[slot], recv_sem=recv.at[slot],
            device_id=peer, device_id_type=pl.DeviceIdType.MESH,
        )
        made.start()
        return made

    pos_f[...] = jnp.zeros_like(pos_f)
    mill_f[...] = jnp.zeros_like(mill_f)
    bias_f[...] = jnp.zeros_like(bias_f)
    miller = mill[...].astype(F32)
    for part, piece in enumerate(split_three(pos[0])):
        pos_f[pl.ds(3 * part, 3), :] = piece
        mill_f[pl.ds(3 * part, 3), :] = miller
    pos_s[...] = pos_f[...].astype(BF)
    mill_s[...] = mill_f[...].astype(BF)
    for part, piece in enumerate(split_three(bias[...])):
        bias_f[pl.ds(16 * part, bias.shape[0]), :] = piece
    bias_s[...] = bias_f[...].astype(BF)
    kinds = lax.rem(lax.broadcasted_iota(jnp.int32, hot.shape, 0), 16)
    own_kind = jnp.broadcast_to(spec[:, pl.ds(pl.multiple_of(x * half, 128), half)], hot.shape)
    hot[...] = (kinds == own_kind).astype(F32).astype(BF)
    eye = (
        lax.broadcasted_iota(jnp.int32, (channels, channels), 0)
        == lax.broadcasted_iota(jnp.int32, (channels, channels), 1)
    ).astype(F32).astype(BF)
    out_t[...] = mul(eye, w_out[...], (1, 1)).astype(BF)
    factor = TWO_PI / jnp.full((1, kv), clen[0], F32)
    square = jnp.sum(miller * miller, axis=0, keepdims=True) * (factor * factor)
    decay = jnp.exp(-0.5 * square) / square * (1.0 / math.sqrt(atoms_total * KVECS))
    cw[:, pl.ds(0, kv)] = decay
    cw[:, pl.ds(kv, kv)] = decay

    @pl.loop(0, half // ROWS)
    def _(i):
        at = pl.ds(pl.multiple_of(i * ROWS, ROWS), ROWS)
        source = pl.ds(pl.multiple_of(x * half + i * ROWS, ROWS), ROWS)
        linear = mul(feat[0, source, :], w_in[...], (1, 0)) + mul(hot[:, at], bias_s[...], (0, 0))
        gate = 0.5 * jnp.tanh(0.5 * linear) + 0.5
        hidden = linear * gate
        slope1[at, :] = gate + hidden * (1.0 - gate)
        hidden = hidden.astype(BF)
        h1[at, :] = hidden
        linear = mul(hidden, w_mid[...], (1, 0))
        gate = 0.5 * jnp.tanh(0.5 * linear) + 0.5
        hidden = linear * gate
        slope2[at, :] = gate + hidden * (1.0 - gate)
        hidden = hidden.astype(BF)
        h2[at, :] = hidden
        ch[x, :, at] = mul(out_t[...], hidden, (1, 1)).astype(BF)

    pl.semaphore_wait(barrier, len(peers))
    charges = copy(ch.at[x], ch.at[x], to_x)

    panels[...] = jnp.zeros_like(panels)

    def phase_half(which):
        @pl.loop(0, half // ROWS)
        def _(i):
            at = pl.ds(pl.multiple_of(i * ROWS, ROWS), ROWS)
            base = pl.multiple_of(which * half + i * ROWS, ROWS)
            turns[...] = mul(pos_s[:, pl.ds(base, ROWS)], mill_s[...], (0, 0))

            @pl.loop(0, ROWS // STRIP, unroll=4)
            def _(j):
                near = turns[pl.ds(pl.multiple_of(j * STRIP, STRIP), STRIP), :]
                near = near - ((near + TURN_SHIFT) - TURN_SHIFT)
                sq = near * near
                sine = near * (SINE[0] + sq * (SINE[1] + sq * (SINE[2] + sq * SINE[3])))
                cosine = COSINE[0] + sq * (COSINE[1] + sq * (COSINE[2] + sq * (COSINE[3] + sq * COSINE[4])))
                to = pl.ds(pl.multiple_of(base + j * STRIP, STRIP), STRIP)
                phases[to, pl.ds(0, kv)] = (1.0 - sine * sine).astype(BF)
                phases[to, pl.ds(kv, kv)] = (sine * cosine).astype(BF)

            panels[...] += mul(ch[which, :, at], phases[pl.ds(base, ROWS), :], (1, 0))

    phase_half(x)
    charges.wait()
    phase_half(1 - x)

    def slab(who):
        return pl.ds(pl.multiple_of(who * width, 128), width)

    sums = []
    for step in range(1, nz):
        pz_s[step] = panels[:, slab(lax.rem(z + step, nz))].astype(BF)
        sums.append(copy(pz_s.at[step], pz_r.at[step], to_z(step)))
    for one in sums:
        one.wait()
    total = panels[:, slab(z)]
    for step in range(1, nz):
        total = total + pz_r[step].astype(F32)
    weighed = total * cw[:, slab(z)]
    w_all[z] = weighed.astype(BF)
    en_mine[...] = jnp.broadcast_to(jnp.sum(total * weighed).reshape(1, 1), en_mine.shape)
    gathers = []
    for step in range(1, nz):
        gathers.append(copy(w_all.at[z], w_all.at[z], to_z(step)))
        gathers.append(copy(en_mine, en_z.at[step], to_z(step)))
    for one in gathers:
        one.wait()
    energy = en_mine[...]
    for step in range(1, nz):
        energy = energy + en_z[step]
    en_sum[...] = energy
    energies = copy(en_sum, en_x, to_x)

    def potential_half(which, store):
        @pl.loop(0, half // ROWS)
        def _(i):
            at = pl.ds(pl.multiple_of(i * ROWS, ROWS), ROWS)
            base = pl.ds(pl.multiple_of(which * half + i * ROWS, ROWS), ROWS)
            value = mul(w_all[0], phases[base, pl.ds(0, width)], (1, 1))
            for who in range(1, nz):
                value = value + mul(w_all[who], phases[base, pl.ds(who * width, width)], (1, 1))
            store[:, at] = value.astype(store.dtype)

    potential_half(1 - x, pot_s)
    others = copy(pot_s, pot_r, to_x)
    potential_half(x, pot)
    energies.wait()
    others.wait()
    energy = (en_sum[...] + en_x[...]) * (1.0 / atoms_total)
    en_o[...] = energy
    scale = (energy[0:1, 0:1] - eref[0]) * (2.0 / atoms_total)
    full = pot[...] + pot_r[...].astype(F32)
    pot[...] = full
    gc[...] = (full * scale).astype(BF)

    @pl.loop(0, half // ROWS)
    def _(i):
        at = pl.ds(pl.multiple_of(i * ROWS, ROWS), ROWS)
        back = mul(gc[:, at], out_t[...], (0, 0))
        g2[at, :] = (back * slope2[at, :]).astype(BF)

    lanes = 128

    def keep(store, first, value):
        for block in range(4):
            store[block, pl.ds(first, value.shape[0]), :] = value[:, block * lanes : (block + 1) * lanes]

    for first in range(0, h1.shape[1], ROWS):
        keep(ga, first, mul(h1[:, pl.ds(first, ROWS)], g2[...], (0, 0)))

    mine = 2 * r + x

    def rep_start(g, out, into):
        out[...] = g[pl.ds(2 * (1 - r), 2)].astype(BF)
        return copy(out, into, to_r)

    def x_start(g, got, out, into):
        out[...] = (g[2 * r + 1 - x] + got[1 - x].astype(F32)).astype(BF)
        return copy(out, into, to_x)

    def z_start(g, got_r, got_x, out, into):
        total = g[mine] + got_r[x].astype(F32) + got_x[...].astype(F32)
        g[mine] = total
        out[...] = total.astype(BF)
        share = out.shape[0] // nz
        made = []
        for step in range(1, nz):
            piece = pl.ds(pl.multiple_of(lax.rem(z + step, nz) * share, 16), share)
            made.append(copy(out.at[piece], into.at[step], to_z(step)))
        return made

    def z_gather(g, got, whole):
        share = got.shape[1]
        piece = pl.ds(pl.multiple_of(z * share, 16), share)
        total = g[mine, piece, :]
        for step in range(1, nz):
            total = total + got[step].astype(F32)
        whole[mine, piece, :] = total.astype(BF)
        return [copy(whole.at[mine, piece], whole.at[mine, piece], to_z(step)) for step in range(1, nz)]

    def finish(made):
        for one in made:
            one.wait()

    rep_a = rep_start(ga, ra_s, ra_r)

    @pl.loop(0, half // ROWS)
    def _(i):
        at = pl.ds(pl.multiple_of(i * ROWS, ROWS), ROWS)
        back = mul(g2[at, :], w_mid[...], (1, 1))
        g1[at, :] = (back * slope1[at, :]).astype(BF)

    rep_a.wait()
    x_a = x_start(ga, ra_r, xa_s, xa_r)
    features_in = feat.shape[2]
    own = pl.ds(pl.multiple_of(x * half, ROWS), half)
    gb[...] = jnp.zeros_like(gb)
    keep(gb, 0, mul(feat[0, own, :], g1[...], (0, 0)))
    keep(gb, features_in, mul(gc[...], h2[...], (1, 0)))
    keep(gb, features_in + channels, mul(hot[pl.ds(0, 16), :], g1[...], (1, 0)))
    rep_b = rep_start(gb, rb_s, rb_r)
    x_a.wait()
    z_a = z_start(ga, ra_r, xa_r, za_s, za_r)
    rep_b.wait()
    x_b = x_start(gb, rb_r, xb_s, xb_r)
    pot_o[...] = pot[...].T
    finish(z_a)
    all_z_a = z_gather(ga, za_r, all_a)
    x_b.wait()
    z_b = z_start(gb, rb_r, xb_r, zb_s, zb_r)
    finish(all_z_a)
    all_x_a = copy(all_a.at[mine], all_a.at[mine], to_x)
    finish(z_b)
    all_z_b = z_gather(gb, zb_r, all_b)
    all_x_a.wait()
    pair = pl.ds(2 * r, 2)
    all_r_a = copy(all_a.at[pair], all_a.at[pair], to_r)
    finish(all_z_b)
    all_x_b = copy(all_b.at[mine], all_b.at[mine], to_x)
    all_r_a.wait()
    for block in range(4):
        gmid_o[:, pl.ds(block * lanes, lanes)] = all_a[block].astype(F32)
    all_x_b.wait()
    all_r_b = copy(all_b.at[pair], all_b.at[pair], to_r)
    all_r_b.wait()
    for block in range(4):
        at = pl.ds(block * lanes, lanes)
        gin_o[:, at] = all_b[block, pl.ds(0, features_in), :].astype(F32)
        gout_o[at, :] = all_b[block, pl.ds(features_in, channels), :].astype(F32).T
        gbias_o[:, at] = all_b[block, pl.ds(features_in + channels, 16), :].astype(F32)[: gbias_o.shape[0]]


def fits(sizes, args):
    atoms, kv = args[0].shape[2], args[5].shape[1]
    nz = sizes["atoms"]
    return (
        sizes["kvec"] == 2
        and sizes["rep"] == 2
        and nz > 1
        and (2 * kv) % (128 * nz) == 0
        and atoms % (2 * ROWS) == 0
        and args[7].shape[0] % (16 * nz) == 0
        and args[7].shape[1] == 512
        and args[9].shape[0] <= 16
    )


def body(sizes, *args):
    if not fits(sizes, args):
        return plain_body(*args)
    positions, features, _, _, _, miller_index, _, weight_mid, weight_out, species_bias = args
    nz = sizes["atoms"]
    atoms, kv = positions.shape[2], miller_index.shape[1]
    half = atoms // 2
    width = 2 * kv // nz
    inner, channels = weight_out.shape
    features_in = features.shape[2]
    rows_a = inner
    rows_b = -(-(features_in + channels + 16) // (16 * nz)) * 16 * nz

    def vmem(*shape, dtype=F32):
        return pltpu.VMEM(shape, dtype)

    def grads(rows):
        return [
            vmem(4, rows, 128),
            vmem(2, rows, 128, dtype=BF), vmem(2, rows, 128, dtype=BF),
            vmem(rows, 128, dtype=BF), vmem(rows, 128, dtype=BF),
            vmem(rows, 128, dtype=BF), vmem(nz, rows // nz, 128, dtype=BF),
            vmem(4, rows, 128, dtype=BF),
        ]

    scratch = [
        vmem(16, atoms), vmem(16, atoms, dtype=BF),
        vmem(16, kv), vmem(16, kv, dtype=BF),
        vmem(48, inner), vmem(48, inner, dtype=BF),
        vmem(48, half, dtype=BF), vmem(channels, inner, dtype=BF), vmem(1, 2 * kv),
        vmem(half, inner, dtype=BF), vmem(half, inner, dtype=BF),
        vmem(half, inner), vmem(half, inner),
        vmem(2, channels, half, dtype=BF), vmem(ROWS, kv), vmem(atoms, 2 * kv, dtype=BF),
        vmem(channels, 2 * kv),
        vmem(nz, channels, width, dtype=BF), vmem(nz, channels, width, dtype=BF),
        vmem(nz, channels, width, dtype=BF),
        vmem(8, 128), vmem(nz, 8, 128), vmem(8, 128), vmem(8, 128),
        vmem(channels, half), vmem(channels, half, dtype=BF), vmem(channels, half, dtype=BF),
        vmem(channels, half, dtype=BF), vmem(half, inner, dtype=BF), vmem(half, inner, dtype=BF),
        *grads(rows_a), *grads(rows_b),
        pltpu.SemaphoreType.DMA((48,)), pltpu.SemaphoreType.DMA((48,)),
    ]
    place = pl.BlockSpec(memory_space=pltpu.VMEM)
    scalar = pl.BlockSpec(memory_space=pltpu.SMEM)
    potential, energy, grad_in, grad_mid, grad_out, grad_bias = pl.pallas_call(
        functools.partial(fused, nz, rows_b),
        out_shape=(
            jax.ShapeDtypeStruct((half, channels), F32),
            jax.ShapeDtypeStruct((8, 128), F32),
            jax.ShapeDtypeStruct((features_in, inner), F32),
            jax.ShapeDtypeStruct((inner, inner), F32),
            jax.ShapeDtypeStruct((inner, channels), F32),
            jax.ShapeDtypeStruct(species_bias.shape, F32),
        ),
        in_specs=[place, place, place, scalar, scalar] + [place] * 5,
        out_specs=[place] * 6,
        scratch_shapes=scratch,
        compiler_params=pltpu.CompilerParams(
            collective_id=0, has_side_effects=True, vmem_limit_bytes=52 * 2**20
        ),
    )(*args)
    return (potential[None], energy[0, :1], grad_in, grad_mid, grad_out, grad_bias)


def solution(mesh):
    placed = (
        P(("groups", "rep"), None, "atoms"),
        P(("groups", "rep"), "atoms", None),
        P(("groups", "rep"), "atoms"),
        P(("groups", "rep")),
        P(("groups", "rep")),
        P(None, "kvec"),
        P(),
        P(),
        P(),
        P(),
    )
    return jax.shard_map(
        functools.partial(body, dict(mesh.shape)),
        mesh=mesh,
        in_specs=placed,
        out_specs=(
            P(("groups", "rep"), ("atoms", "kvec"), None),
            P(("groups", "rep")),
            P("groups", None),
            P("groups", None),
            P("groups", None),
            P("groups", None),
        ),
        check_vma=False,
    )
```

```python
import functools
import math

import jax
import jax.numpy as jnp
from jax import lax
from jax.experimental import pallas as pl
from jax.experimental.pallas import tpu as pltpu
from jax.sharding import PartitionSpec as P

KVECS = 2048


TWO_PI = 2.0 * math.pi
HIGHEST = lax.Precision.HIGHEST


def phase_tiles(coord_rows, miller_float):
    phase_turns = (
        coord_rows[0][:, None] * miller_float[0][None, :]
        + coord_rows[1][:, None] * miller_float[1][None, :]
        + coord_rows[2][:, None] * miller_float[2][None, :]
    )
    phase_angle = TWO_PI * phase_turns
    return jnp.concatenate([jnp.cos(phase_angle), jnp.sin(phase_angle)], axis=1).astype(
        jnp.bfloat16
    )


def wave_weights(miller_float, cell_size, atoms_total):
    index_square = (
        miller_float[0] * miller_float[0]
        + miller_float[1] * miller_float[1]
        + miller_float[2] * miller_float[2]
    )
    factor = TWO_PI / cell_size
    wave_square = index_square * (factor * factor)
    decay_base = jnp.exp(-0.5 * wave_square) / wave_square * (1.0 / math.sqrt(atoms_total * KVECS))
    return jnp.concatenate([decay_base, decay_base])


def contract_rows(left_rows, right_rows):
    return lax.dot_general(
        left_rows, right_rows, (((0,), (0,)), ((), ())), preferred_element_type=jnp.float32
    )


def silu_slope(linear):
    sigmoid_value = jax.nn.sigmoid(linear)
    return sigmoid_value * (1.0 + linear * (1.0 - sigmoid_value))


def forward(atom_features, atom_species, weight_in, weight_mid, weight_out, species_bias):
    kinds = jnp.arange(species_bias.shape[0], dtype=jnp.int32)
    onehot = (atom_species[:, None] == kinds[None, :]).astype(jnp.float32)
    bias_rows = jnp.dot(onehot, species_bias, precision=HIGHEST, preferred_element_type=jnp.float32)
    linear_one = jnp.dot(atom_features, weight_in, preferred_element_type=jnp.float32) + bias_rows
    hidden_one = jax.nn.silu(linear_one).astype(jnp.bfloat16)
    linear_two = jnp.dot(hidden_one, weight_mid, preferred_element_type=jnp.float32)
    hidden_two = jax.nn.silu(linear_two).astype(jnp.bfloat16)
    charges = jnp.dot(hidden_two, weight_out, preferred_element_type=jnp.float32).astype(
        jnp.bfloat16
    )
    return (onehot, linear_one, hidden_one, linear_two, hidden_two, charges)


def backward(
    atom_features,
    onehot,
    linear_one,
    hidden_one,
    linear_two,
    hidden_two,
    grad_charges,
    weight_mid,
    weight_out,
):
    grad_out = contract_rows(hidden_two, grad_charges)
    back_two = lax.dot_general(
        grad_charges, weight_out, (((1,), (1,)), ((), ())), preferred_element_type=jnp.float32
    )
    grad_two = (back_two * silu_slope(linear_two)).astype(jnp.bfloat16)
    grad_mid = contract_rows(hidden_one, grad_two)
    back_one = lax.dot_general(
        grad_two, weight_mid, (((1,), (1,)), ((), ())), preferred_element_type=jnp.float32
    )
    grad_one = (back_one * silu_slope(linear_one)).astype(jnp.bfloat16)
    grad_in = contract_rows(atom_features, grad_one)
    grad_bias = contract_rows(onehot.astype(jnp.bfloat16), grad_one)
    return (grad_in, grad_mid, grad_out, grad_bias)


def plain_body(
    positions,
    features,
    species,
    cell_length,
    energy_ref,
    miller_index,
    weight_in,
    weight_mid,
    weight_out,
    species_bias,
):
    block_rows = positions.shape[2]
    kvec_count = miller_index.shape[1]
    channels = weight_out.shape[1]
    atoms_total = block_rows * lax.axis_size("atoms")
    quarter = block_rows // lax.axis_size("kvec")
    own_first = lax.axis_index("kvec") * quarter
    miller_float = miller_index.astype(jnp.float32)
    column_weights = wave_weights(miller_float, cell_length[0], atoms_total)
    coords = positions[0]
    step_rows = math.gcd(block_rows, 512)
    stored = jnp.concatenate(
        [
            phase_tiles(lax.slice_in_dim(coords, offset, offset + step_rows, axis=1), miller_float)
            for offset in range(0, block_rows, step_rows)
        ],
        axis=0,
    )

    def tile_rows(first_row, row_count):
        return lax.dynamic_slice_in_dim(stored, first_row, row_count, 0)

    zero_panels = jnp.zeros((channels, 2 * kvec_count), jnp.float32)
    own_features = features[0]
    own_species = species[0]
    onehot, linear_one, hidden_one, linear_two, hidden_two, charges = forward(
        own_features, own_species, weight_in, weight_mid, weight_out, species_bias
    )
    running = zero_panels
    row_count = charges.shape[0]
    piece_rows = math.gcd(row_count, 512)
    for inner_start in range(0, row_count, piece_rows):
        phase_rows = tile_rows(0 + inner_start, piece_rows)
        running = running + contract_rows(
            lax.slice_in_dim(charges, inner_start, inner_start + piece_rows, axis=0), phase_rows
        )
    summed = lax.psum(running, "atoms")
    energy_sum = lax.psum(jnp.sum(summed * summed * column_weights[None, :]).reshape(1), "kvec")
    weighted = (summed * column_weights[None, :]).astype(jnp.bfloat16)
    energy = energy_sum / atoms_total
    piece_rows = math.gcd(block_rows, 512)
    pieces = []
    for inner_start in range(0, block_rows, piece_rows):
        phase_rows = tile_rows(0 + inner_start, piece_rows)
        pieces.append(
            lax.dot_general(
                phase_rows, weighted, (((1,), (1,)), ((), ())), preferred_element_type=jnp.float32
            )
        )
    used_potential = lax.psum(jnp.concatenate(pieces, axis=0), "kvec")
    own_potential = lax.dynamic_slice_in_dim(used_potential, own_first, quarter, 0)
    loss_scale = (energy[0] - energy_ref[0]) * (2.0 / atoms_total)
    grad_charges = (loss_scale * used_potential).astype(jnp.bfloat16)
    local_in, local_mid, local_out, local_bias = backward(
        own_features,
        onehot,
        linear_one,
        hidden_one,
        linear_two,
        hidden_two,
        grad_charges,
        weight_mid,
        weight_out,
    )
    grad_in, grad_mid, grad_out, grad_bias = lax.psum(
        (local_in, local_mid, local_out, local_bias), ("atoms", "rep")
    )
    return (own_potential[None], energy, grad_in, grad_mid, grad_out, grad_bias)


TURN_SHIFT = 1.5 * 2.0**23
SINE = (4.442867834, -7.307441175, 3.594769894, -0.784331973)
COSINE = (1.414213496, -6.978850946, 5.739460314, -1.883557438, 0.310686957)
ROWS = 256
STRIP = 16
BF = jnp.bfloat16
F32 = jnp.float32


def mul(left, right, dims):
    return lax.dot_general(left, right, ((dims[:1], dims[1:]), ((), ())), preferred_element_type=F32)


def split_three(value):
    high = value.astype(BF).astype(F32)
    rest = value - high
    middle = rest.astype(BF).astype(F32)
    return high, middle, rest - middle


def fused(
    nz, rows_b,
    pos, feat, spec, clen, eref, mill, w_in, w_mid, out_t, bias,
    pot, en_o, all_0, all_1, all_2,
    pos_f, pos_s, mill_f, mill_s, bias_f, bias_s, hot, cw,
    h1, h2, slope1, slope2, ch, turns, phases, panels,
    pz_s, pz_r, w_all, en_mine, en_z, en_x, en_sum,
    pot_s, pot_r, gc, g2, g1,
    *rest,
):
    send, recv = rest[-2:]
    chunks = [(*rest[7 * c : 7 * c + 7], whole) for c, whole in enumerate((all_0, all_1, all_2))]
    z = lax.axis_index("atoms")
    x = lax.axis_index("kvec")
    r = lax.axis_index("rep")
    atoms = pos.shape[2]
    half = atoms // 2
    kv = mill.shape[1]
    channels = out_t.shape[0]
    width = 2 * kv // nz
    atoms_total = atoms * nz
    to_x = {"kvec": 1 - x}
    to_r = {"rep": 1 - r}

    def to_z(step):
        return {"atoms": lax.rem(z + step, nz)}

    barrier = pltpu.get_barrier_semaphore()
    peers = [to_x, to_r] + [to_z(step) for step in range(1, nz)]
    for peer in peers:
        pl.semaphore_signal(barrier, inc=1, device_id=peer, device_id_type=pl.DeviceIdType.MESH)

    count = [0]

    def copy(src, dst, peer):
        slot = count[0]
        count[0] += 1
        made = pltpu.make_async_remote_copy(
            src_ref=src, dst_ref=dst, send_sem=send.at[slot], recv_sem=recv.at[slot],
            device_id=peer, device_id_type=pl.DeviceIdType.MESH,
        )
        made.start()
        return made

    pos_f[...] = jnp.zeros_like(pos_f)
    mill_f[...] = jnp.zeros_like(mill_f)
    bias_f[...] = jnp.zeros_like(bias_f)
    miller = mill[...].astype(F32)
    for part in range(3):
        mill_f[pl.ds(3 * part, 3), :] = miller
    for axis in range(3):
        for part, piece in enumerate(split_three(pos[axis])):
            pos_f[pl.ds(3 * part + axis, 1), :] = piece
    pos_s[...] = pos_f[...].astype(BF)
    mill_s[...] = mill_f[...].astype(BF)
    for part, piece in enumerate(split_three(bias[...])):
        bias_f[pl.ds(16 * part, bias.shape[0]), :] = piece
    bias_s[...] = bias_f[...].astype(BF)
    kinds = lax.rem(lax.broadcasted_iota(jnp.int32, hot.shape, 0), 16)
    own_kind = jnp.broadcast_to(spec[:, pl.ds(pl.multiple_of(x * half, 128), half)], hot.shape)
    hot[...] = (kinds == own_kind).astype(F32).astype(BF)
    factor = TWO_PI / jnp.full((1, kv), clen[0], F32)
    square = jnp.sum(miller * miller, axis=0, keepdims=True) * (factor * factor)
    decay = jnp.exp(-0.5 * square) / square * (1.0 / math.sqrt(atoms_total * KVECS))
    cw[:, pl.ds(0, kv)] = decay
    cw[:, pl.ds(kv, kv)] = decay

    @pl.loop(0, half // ROWS)
    def _(i):
        at = pl.ds(pl.multiple_of(i * ROWS, ROWS), ROWS)
        source = pl.ds(pl.multiple_of(x * half + i * ROWS, ROWS), ROWS)
        linear = mul(feat[0, source, :], w_in[...], (1, 0)) + mul(hot[:, at], bias_s[...], (0, 0))
        gate = 0.5 * jnp.tanh(0.5 * linear) + 0.5
        hidden = linear * gate
        slope1[at, :] = gate + hidden * (1.0 - gate)
        hidden = hidden.astype(BF)
        h1[at, :] = hidden
        linear = mul(hidden, w_mid[...], (1, 0))
        gate = 0.5 * jnp.tanh(0.5 * linear) + 0.5
        hidden = linear * gate
        slope2[at, :] = gate + hidden * (1.0 - gate)
        hidden = hidden.astype(BF)
        h2[at, :] = hidden
        ch[x, :, at] = mul(out_t[...], hidden, (1, 1)).astype(BF)

    panels[...] = jnp.zeros_like(panels)

    def phase_tile(base):
        turns[...] = mul(pos_s[:, pl.ds(base, ROWS)], mill_s[...], (0, 0))

        @pl.loop(0, ROWS // STRIP, unroll=4)
        def _(j):
            near = turns[pl.ds(pl.multiple_of(j * STRIP, STRIP), STRIP), :]
            near = near - ((near + TURN_SHIFT) - TURN_SHIFT)
            sq = near * near
            sine = near * (SINE[0] + sq * (SINE[1] + sq * (SINE[2] + sq * SINE[3])))
            cosine = COSINE[0] + sq * (COSINE[1] + sq * (COSINE[2] + sq * (COSINE[3] + sq * COSINE[4])))
            to = pl.ds(pl.multiple_of(base + j * STRIP, STRIP), STRIP)
            phases[to, pl.ds(0, kv)] = (1.0 - sine * sine).astype(BF)
            phases[to, pl.ds(kv, kv)] = (sine * cosine).astype(BF)

    def panel_half(which):
        @pl.loop(0, half // (2 * ROWS))
        def _(i):
            at = pl.ds(pl.multiple_of(i * 2 * ROWS, ROWS), 2 * ROWS)
            base = pl.ds(pl.multiple_of(which * half + i * 2 * ROWS, ROWS), 2 * ROWS)
            panels[...] += mul(ch[which, :, at], phases[base, :], (1, 0))

    def phase_half(which):
        @pl.loop(0, half // ROWS)
        def _(i):
            phase_tile(pl.multiple_of(which * half + i * ROWS, ROWS))

    phase_half(x)
    pl.semaphore_wait(barrier, len(peers))
    charges = copy(ch.at[x], ch.at[x], to_x)
    panel_half(x)
    phase_half(1 - x)
    charges.wait()
    panel_half(1 - x)

    def slab(who):
        return pl.ds(pl.multiple_of(who * width, 128), width)

    sums = []
    for step in range(1, nz):
        pz_s[step] = panels[:, slab(lax.rem(z + step, nz))].astype(BF)
        sums.append(copy(pz_s.at[step], pz_r.at[step], to_z(step)))
    for one in sums:
        one.wait()
    total = panels[:, slab(z)]
    for step in range(1, nz):
        total = total + pz_r[step].astype(F32)
    weighed = total * cw[:, slab(z)]
    w_all[z] = weighed.astype(BF)
    en_mine[...] = jnp.broadcast_to(jnp.sum(total * weighed).reshape(1, 1), en_mine.shape)
    gathers = [copy(w_all.at[z], w_all.at[z], to_z(step)) for step in range(1, nz)]
    shares = [copy(en_mine, en_z.at[step], to_z(step)) for step in range(1, nz)]
    for one in gathers:
        one.wait()

    def potential_half(which, store):
        @pl.loop(0, half // ROWS)
        def _(i):
            at = pl.ds(pl.multiple_of(i * ROWS, ROWS), ROWS)
            base = pl.ds(pl.multiple_of(which * half + i * ROWS, ROWS), ROWS)
            value = mul(w_all[0], phases[base, pl.ds(0, width)], (1, 1))
            for who in range(1, nz):
                value = value + mul(w_all[who], phases[base, pl.ds(who * width, width)], (1, 1))
            store[:, at] = value.astype(store.dtype)

    potential_half(1 - x, pot_s)
    others = copy(pot_s, pot_r, to_x)
    for one in shares:
        one.wait()
    energy = en_mine[...]
    for step in range(1, nz):
        energy = energy + en_z[step]
    en_sum[...] = energy
    energies = copy(en_sum, en_x, to_x)
    potential_half(x, pot)
    energies.wait()
    others.wait()
    energy = (en_sum[...] + en_x[...]) * (1.0 / atoms_total)
    en_o[...] = energy
    scale = (energy[0:1, 0:1] - eref[0]) * (2.0 / atoms_total)
    full = pot[...] + pot_r[...].astype(F32)
    pot[...] = full
    gc[...] = (full * scale).astype(BF)

    @pl.loop(0, half // ROWS)
    def _(i):
        at = pl.ds(pl.multiple_of(i * ROWS, ROWS), ROWS)
        back = mul(gc[:, at], out_t[...], (0, 0))
        g2[at, :] = (back * slope2[at, :]).astype(BF)

    lanes = 128

    def keep(store, first, value):
        for block in range(4):
            store[block, pl.ds(first, value.shape[0]), :] = value[:, block * lanes : (block + 1) * lanes]

    mine = 2 * r + x

    def rep_start(g, out, into):
        out[...] = g[pl.ds(2 * (1 - r), 2)].astype(BF)
        return copy(out, into, to_r)

    def x_start(g, got, out, into):
        out[...] = (g[2 * r + 1 - x] + got[1 - x].astype(F32)).astype(BF)
        return copy(out, into, to_x)

    def z_start(g, got_r, got_x, out, into):
        total = g[mine] + got_r[x].astype(F32) + got_x[...].astype(F32)
        g[mine] = total
        out[...] = total.astype(BF)
        share = out.shape[0] // nz
        made = []
        for step in range(1, nz):
            piece = pl.ds(pl.multiple_of(lax.rem(z + step, nz) * share, 16), share)
            made.append(copy(out.at[piece], into.at[step], to_z(step)))
        return made

    def z_gather(g, got, whole):
        share = got.shape[1]
        piece = pl.ds(pl.multiple_of(z * share, 16), share)
        total = g[mine, piece, :]
        for step in range(1, nz):
            total = total + got[step].astype(F32)
        whole[mine, piece, :] = total.astype(BF)
        return [copy(whole.at[mine, piece], whole.at[mine, piece], to_z(step)) for step in range(1, nz)]

    def finish(made):
        for one in made:
            one.wait()

    def swap_pair(c):
        g, out, into = chunks[c][:3]
        return rep_start(g, out, into)

    def swap_x(c):
        g, _, got, out, into = chunks[c][:5]
        return x_start(g, got, out, into)

    def scatter(c):
        g, _, got_r, _, got_x, out, into, _ = chunks[c]
        return z_start(g, got_r, got_x, out, into)

    def gather(c):
        g, _, _, _, _, _, got, whole = chunks[c]
        return z_gather(g, got, whole)

    def gather_x(c):
        whole = chunks[c][7]
        return copy(whole.at[mine], whole.at[mine], to_x)

    def gather_pair(c):
        whole = chunks[c][7]
        pair = pl.ds(2 * r, 2)
        return copy(whole.at[pair], whole.at[pair], to_r)

    part = h1.shape[1] // 2
    keep(chunks[0][0], 0, mul(h1[:, pl.ds(0, part)], g2[...], (0, 0)))
    pair_0 = swap_pair(0)
    keep(chunks[1][0], 0, mul(h1[:, pl.ds(part, part)], g2[...], (0, 0)))
    pair_1 = swap_pair(1)

    @pl.loop(0, half // ROWS)
    def _(i):
        at = pl.ds(pl.multiple_of(i * ROWS, ROWS), ROWS)
        back = mul(g2[at, :], w_mid[...], (1, 1))
        g1[at, :] = (back * slope1[at, :]).astype(BF)

    pair_0.wait()
    x_0 = swap_x(0)
    pair_1.wait()
    x_1 = swap_x(1)
    features_in = feat.shape[2]
    own = pl.ds(pl.multiple_of(x * half, ROWS), half)
    last = chunks[2][0]
    last[...] = jnp.zeros_like(last)
    keep(last, 0, mul(feat[0, own, :], g1[...], (0, 0)))
    keep(last, features_in, mul(gc[...], h2[...], (1, 0)))
    keep(last, features_in + channels, mul(hot[pl.ds(0, 16), :], g1[...], (1, 0)))
    pair_2 = swap_pair(2)
    x_0.wait()
    z_0 = scatter(0)
    pair_2.wait()
    x_2 = swap_x(2)
    x_1.wait()
    z_1 = scatter(1)
    finish(z_0)
    gz_0 = gather(0)
    x_2.wait()
    z_2 = scatter(2)
    finish(z_1)
    gz_1 = gather(1)
    finish(gz_0)
    gx_0 = gather_x(0)
    finish(z_2)
    gz_2 = gather(2)
    finish(gz_1)
    gx_1 = gather_x(1)
    gx_0.wait()
    gr_0 = gather_pair(0)
    finish(gz_2)
    gx_2 = gather_x(2)
    gx_1.wait()
    gr_1 = gather_pair(1)
    gx_2.wait()
    gr_2 = gather_pair(2)
    finish([gr_0, gr_1, gr_2])


def write(features_in, pot, energy, all_0, all_1, all_2, pot_o, en_o, gin_o, gmid_o, gout_o, gbias_o):
    channels = pot.shape[0]
    part = all_0.shape[1]
    en_o[0] = energy[0, 0]
    pot_o[0] = pot[...]
    for block in range(4):
        at = pl.ds(block * 128, 128)
        gmid_o[pl.ds(0, part), at] = all_0[block].astype(F32)
        gmid_o[pl.ds(part, part), at] = all_1[block].astype(F32)
        gin_o[:, at] = all_2[block, pl.ds(0, features_in), :].astype(F32)
        gout_o[:, at] = all_2[block, pl.ds(features_in, channels), :].astype(F32)
        bias_rows = all_2[block, pl.ds(features_in + channels, 16), :].astype(F32)
        gbias_o[:, at] = bias_rows[: gbias_o.shape[0]]


def fits(sizes, args):
    atoms, kv = args[0].shape[2], args[5].shape[1]
    nz = sizes["atoms"]
    return (
        sizes["kvec"] == 2
        and sizes["rep"] == 2
        and nz > 1
        and (2 * kv) % (128 * nz) == 0
        and atoms % (2 * ROWS) == 0
        and args[7].shape[0] % (32 * nz) == 0
        and args[7].shape[1] == 512
        and args[9].shape[0] <= 16
    )


def body(sizes, *args):
    if not fits(sizes, args):
        return plain_body(*args)
    positions, features, _, _, _, miller_index, _, weight_mid, weight_out, species_bias = args
    nz = sizes["atoms"]
    atoms, kv = positions.shape[2], miller_index.shape[1]
    half = atoms // 2
    width = 2 * kv // nz
    inner, channels = weight_out.shape
    features_in = features.shape[2]
    rows_a = inner // 2
    rows_b = -(-(features_in + channels + 16) // (16 * nz)) * 16 * nz

    def vmem(*shape, dtype=F32):
        return pltpu.VMEM(shape, dtype)

    def grads(rows):
        return [
            vmem(4, rows, 128),
            vmem(2, rows, 128, dtype=BF), vmem(2, rows, 128, dtype=BF),
            vmem(rows, 128, dtype=BF), vmem(rows, 128, dtype=BF),
            vmem(rows, 128, dtype=BF), vmem(nz, rows // nz, 128, dtype=BF),
        ]

    scratch = [
        vmem(16, atoms), vmem(16, atoms, dtype=BF),
        vmem(16, kv), vmem(16, kv, dtype=BF),
        vmem(48, inner), vmem(48, inner, dtype=BF),
        vmem(48, half, dtype=BF), vmem(1, 2 * kv),
        vmem(half, inner, dtype=BF), vmem(half, inner, dtype=BF),
        vmem(half, inner), vmem(half, inner),
        vmem(2, channels, half, dtype=BF), vmem(ROWS, kv), vmem(atoms, 2 * kv, dtype=BF),
        vmem(channels, 2 * kv),
        vmem(nz, channels, width, dtype=BF), vmem(nz, channels, width, dtype=BF),
        vmem(nz, channels, width, dtype=BF),
        vmem(8, 128), vmem(nz, 8, 128), vmem(8, 128), vmem(8, 128),
        vmem(channels, half, dtype=BF), vmem(channels, half, dtype=BF),
        vmem(channels, half, dtype=BF), vmem(half, inner, dtype=BF), vmem(half, inner, dtype=BF),
        *grads(rows_a), *grads(rows_a), *grads(rows_b),
        pltpu.SemaphoreType.DMA((56,)), pltpu.SemaphoreType.DMA((56,)),
    ]
    place = pl.BlockSpec(memory_space=pltpu.VMEM)
    scalar = pl.BlockSpec(memory_space=pltpu.SMEM)
    found = pl.pallas_call(
        functools.partial(fused, nz, rows_b),
        out_shape=(
            jax.ShapeDtypeStruct((channels, half), F32),
            jax.ShapeDtypeStruct((8, 128), F32),
            jax.ShapeDtypeStruct((4, rows_a, 128), BF),
            jax.ShapeDtypeStruct((4, rows_a, 128), BF),
            jax.ShapeDtypeStruct((4, rows_b, 128), BF),
        ),
        in_specs=[place, place, place, scalar, scalar] + [place] * 5,
        out_specs=[place] * 5,
        scratch_shapes=scratch,
        compiler_params=pltpu.CompilerParams(
            collective_id=0, has_side_effects=True, vmem_limit_bytes=52 * 2**20
        ),
    )(jnp.swapaxes(positions, 0, 1), *args[1:8], weight_out.T, species_bias)
    potential, energy, grad_in, grad_mid, grad_out, grad_bias = (
        pl.pallas_call(
            functools.partial(write, features_in),
            out_shape=(
                jax.ShapeDtypeStruct((1, channels, half), F32),
                jax.ShapeDtypeStruct((1,), F32),
                jax.ShapeDtypeStruct((features_in, inner), F32),
                jax.ShapeDtypeStruct((inner, inner), F32),
                jax.ShapeDtypeStruct((channels, inner), F32),
                jax.ShapeDtypeStruct(species_bias.shape, F32),
            ),
            in_specs=[place] * 5,
            out_specs=[place, scalar] + [place] * 4,
            compiler_params=pltpu.CompilerParams(vmem_limit_bytes=16 * 2**20),
        )(*found)
    )
    return (jnp.swapaxes(potential, 1, 2), energy, grad_in, grad_mid, grad_out.T, grad_bias)


def solution(mesh):
    placed = (
        P(("groups", "rep"), None, "atoms"),
        P(("groups", "rep"), "atoms", None),
        P(("groups", "rep"), "atoms"),
        P(("groups", "rep")),
        P(("groups", "rep")),
        P(None, "kvec"),
        P(),
        P(),
        P(),
        P(),
    )
    return jax.shard_map(
        functools.partial(body, dict(mesh.shape)),
        mesh=mesh,
        in_specs=placed,
        out_specs=(
            P(("groups", "rep"), ("atoms", "kvec"), None),
            P(("groups", "rep")),
            P("groups", None),
            P("groups", None),
            P("groups", None),
            P("groups", None),
        ),
        check_vma=False,
    )
```

```python
import functools
import math

import jax
import jax.numpy as jnp
from jax import lax
from jax.experimental import pallas as pl
from jax.experimental.pallas import tpu as pltpu
from jax.sharding import PartitionSpec as P

KVECS = 2048


TWO_PI = 2.0 * math.pi
HIGHEST = lax.Precision.HIGHEST


def phase_tiles(coord_rows, miller_float):
    phase_turns = (
        coord_rows[0][:, None] * miller_float[0][None, :]
        + coord_rows[1][:, None] * miller_float[1][None, :]
        + coord_rows[2][:, None] * miller_float[2][None, :]
    )
    phase_angle = TWO_PI * phase_turns
    return jnp.concatenate([jnp.cos(phase_angle), jnp.sin(phase_angle)], axis=1).astype(
        jnp.bfloat16
    )


def wave_weights(miller_float, cell_size, atoms_total):
    index_square = (
        miller_float[0] * miller_float[0]
        + miller_float[1] * miller_float[1]
        + miller_float[2] * miller_float[2]
    )
    factor = TWO_PI / cell_size
    wave_square = index_square * (factor * factor)
    decay_base = jnp.exp(-0.5 * wave_square) / wave_square * (1.0 / math.sqrt(atoms_total * KVECS))
    return jnp.concatenate([decay_base, decay_base])


def contract_rows(left_rows, right_rows):
    return lax.dot_general(
        left_rows, right_rows, (((0,), (0,)), ((), ())), preferred_element_type=jnp.float32
    )


def silu_slope(linear):
    sigmoid_value = jax.nn.sigmoid(linear)
    return sigmoid_value * (1.0 + linear * (1.0 - sigmoid_value))


def forward(atom_features, atom_species, weight_in, weight_mid, weight_out, species_bias):
    kinds = jnp.arange(species_bias.shape[0], dtype=jnp.int32)
    onehot = (atom_species[:, None] == kinds[None, :]).astype(jnp.float32)
    bias_rows = jnp.dot(onehot, species_bias, precision=HIGHEST, preferred_element_type=jnp.float32)
    linear_one = jnp.dot(atom_features, weight_in, preferred_element_type=jnp.float32) + bias_rows
    hidden_one = jax.nn.silu(linear_one).astype(jnp.bfloat16)
    linear_two = jnp.dot(hidden_one, weight_mid, preferred_element_type=jnp.float32)
    hidden_two = jax.nn.silu(linear_two).astype(jnp.bfloat16)
    charges = jnp.dot(hidden_two, weight_out, preferred_element_type=jnp.float32).astype(
        jnp.bfloat16
    )
    return (onehot, linear_one, hidden_one, linear_two, hidden_two, charges)


def backward(
    atom_features,
    onehot,
    linear_one,
    hidden_one,
    linear_two,
    hidden_two,
    grad_charges,
    weight_mid,
    weight_out,
):
    grad_out = contract_rows(hidden_two, grad_charges)
    back_two = lax.dot_general(
        grad_charges, weight_out, (((1,), (1,)), ((), ())), preferred_element_type=jnp.float32
    )
    grad_two = (back_two * silu_slope(linear_two)).astype(jnp.bfloat16)
    grad_mid = contract_rows(hidden_one, grad_two)
    back_one = lax.dot_general(
        grad_two, weight_mid, (((1,), (1,)), ((), ())), preferred_element_type=jnp.float32
    )
    grad_one = (back_one * silu_slope(linear_one)).astype(jnp.bfloat16)
    grad_in = contract_rows(atom_features, grad_one)
    grad_bias = contract_rows(onehot.astype(jnp.bfloat16), grad_one)
    return (grad_in, grad_mid, grad_out, grad_bias)


def plain_body(
    positions,
    features,
    species,
    cell_length,
    energy_ref,
    miller_index,
    weight_in,
    weight_mid,
    weight_out,
    species_bias,
):
    block_rows = positions.shape[2]
    kvec_count = miller_index.shape[1]
    channels = weight_out.shape[1]
    atoms_total = block_rows * lax.axis_size("atoms")
    quarter = block_rows // lax.axis_size("kvec")
    own_first = lax.axis_index("kvec") * quarter
    miller_float = miller_index.astype(jnp.float32)
    column_weights = wave_weights(miller_float, cell_length[0], atoms_total)
    coords = positions[0]
    step_rows = math.gcd(block_rows, 512)
    stored = jnp.concatenate(
        [
            phase_tiles(lax.slice_in_dim(coords, offset, offset + step_rows, axis=1), miller_float)
            for offset in range(0, block_rows, step_rows)
        ],
        axis=0,
    )

    def tile_rows(first_row, row_count):
        return lax.dynamic_slice_in_dim(stored, first_row, row_count, 0)

    zero_panels = jnp.zeros((channels, 2 * kvec_count), jnp.float32)
    own_features = features[0]
    own_species = species[0]
    onehot, linear_one, hidden_one, linear_two, hidden_two, charges = forward(
        own_features, own_species, weight_in, weight_mid, weight_out, species_bias
    )
    running = zero_panels
    row_count = charges.shape[0]
    piece_rows = math.gcd(row_count, 512)
    for inner_start in range(0, row_count, piece_rows):
        phase_rows = tile_rows(0 + inner_start, piece_rows)
        running = running + contract_rows(
            lax.slice_in_dim(charges, inner_start, inner_start + piece_rows, axis=0), phase_rows
        )
    summed = lax.psum(running, "atoms")
    energy_sum = lax.psum(jnp.sum(summed * summed * column_weights[None, :]).reshape(1), "kvec")
    weighted = (summed * column_weights[None, :]).astype(jnp.bfloat16)
    energy = energy_sum / atoms_total
    piece_rows = math.gcd(block_rows, 512)
    pieces = []
    for inner_start in range(0, block_rows, piece_rows):
        phase_rows = tile_rows(0 + inner_start, piece_rows)
        pieces.append(
            lax.dot_general(
                phase_rows, weighted, (((1,), (1,)), ((), ())), preferred_element_type=jnp.float32
            )
        )
    used_potential = lax.psum(jnp.concatenate(pieces, axis=0), "kvec")
    own_potential = lax.dynamic_slice_in_dim(used_potential, own_first, quarter, 0)
    loss_scale = (energy[0] - energy_ref[0]) * (2.0 / atoms_total)
    grad_charges = (loss_scale * used_potential).astype(jnp.bfloat16)
    local_in, local_mid, local_out, local_bias = backward(
        own_features,
        onehot,
        linear_one,
        hidden_one,
        linear_two,
        hidden_two,
        grad_charges,
        weight_mid,
        weight_out,
    )
    grad_in, grad_mid, grad_out, grad_bias = lax.psum(
        (local_in, local_mid, local_out, local_bias), ("atoms", "rep")
    )
    return (own_potential[None], energy, grad_in, grad_mid, grad_out, grad_bias)


TURN_SHIFT = 1.5 * 2.0**23
SINE = (4.442867834, -7.307441175, 3.594769894, -0.784331973)
COSINE = (1.414213496, -6.978850946, 5.739460314, -1.883557438, 0.310686957)
ROWS = 256
STRIP = 16
BF = jnp.bfloat16
F32 = jnp.float32


def mul(left, right, dims):
    return lax.dot_general(left, right, ((dims[:1], dims[1:]), ((), ())), preferred_element_type=F32)


def split_three(value):
    high = value.astype(BF).astype(F32)
    rest = value - high
    middle = rest.astype(BF).astype(F32)
    return high, middle, rest - middle


def fused(
    nz, rows_b,
    pos_h, feat_h, spec_h, clen, eref, mill_h, w_in_h, w_mid_h, out_h, bias_h,
    pot, en_o, all_0, all_1, all_2,
    pos, feat, spec, mill, w_in, w_mid, out_t, bias,
    pos_f, pos_s, mill_f, mill_s, bias_f, bias_s, hot, cw,
    h1, h2, slope1, slope2, ch, turns, phases, panels,
    pz_s, pz_r, w_all, en_mine, en_z, en_x, en_sum,
    pot_s, pot_r, gc, g2, g1,
    *rest,
):
    send, recv, load = rest[-3:]
    chunks = [(*rest[7 * c : 7 * c + 7], whole) for c, whole in enumerate((all_0, all_1, all_2))]
    z = lax.axis_index("atoms")
    x = lax.axis_index("kvec")
    r = lax.axis_index("rep")
    atoms = pos_h.shape[2]
    half = atoms // 2
    kv = mill.shape[1]
    channels = out_t.shape[0]
    width = 2 * kv // nz
    atoms_total = atoms * nz
    to_x = {"kvec": 1 - x}
    to_r = {"rep": 1 - r}

    def to_z(step):
        return {"atoms": lax.rem(z + step, nz)}

    own_rows = pl.ds(pl.multiple_of(x * half, ROWS), half)
    pairs = (
        (pos_h, pos), (mill_h, mill), (bias_h, bias), (spec_h, spec),
        (feat_h.at[0, own_rows], feat), (w_in_h, w_in), (w_mid_h, w_mid), (out_h, out_t),
    )
    loads = [pltpu.make_async_copy(src, dst, load.at[i]) for i, (src, dst) in enumerate(pairs)]
    barrier = pltpu.get_barrier_semaphore()
    peers = [to_x, to_r] + [to_z(step) for step in range(1, nz)]
    for peer in peers:
        pl.semaphore_signal(barrier, inc=1, device_id=peer, device_id_type=pl.DeviceIdType.MESH)

    for one in loads:
        one.start()

    count = [0]

    def copy(src, dst, peer):
        slot = count[0]
        count[0] += 1
        made = pltpu.make_async_remote_copy(
            src_ref=src, dst_ref=dst, send_sem=send.at[slot], recv_sem=recv.at[slot],
            device_id=peer, device_id_type=pl.DeviceIdType.MESH,
        )
        made.start()
        return made

    for one in loads[:4]:
        one.wait()

    pos_f[...] = jnp.zeros_like(pos_f)
    mill_f[...] = jnp.zeros_like(mill_f)
    bias_f[...] = jnp.zeros_like(bias_f)
    miller = mill[...].astype(F32)
    for part in range(3):
        mill_f[pl.ds(3 * part, 3), :] = miller
    for axis in range(3):
        for part, piece in enumerate(split_three(pos[axis])):
            pos_f[pl.ds(3 * part + axis, 1), :] = piece
    pos_s[...] = pos_f[...].astype(BF)
    mill_s[...] = mill_f[...].astype(BF)
    for part, piece in enumerate(split_three(bias[...])):
        bias_f[pl.ds(16 * part, bias.shape[0]), :] = piece
    bias_s[...] = bias_f[...].astype(BF)
    kinds = lax.rem(lax.broadcasted_iota(jnp.int32, hot.shape, 0), 16)
    own_kind = jnp.broadcast_to(spec[:, pl.ds(pl.multiple_of(x * half, 128), half)], hot.shape)
    hot[...] = (kinds == own_kind).astype(F32).astype(BF)
    factor = TWO_PI / jnp.full((1, kv), clen[0], F32)
    square = jnp.sum(miller * miller, axis=0, keepdims=True) * (factor * factor)
    decay = jnp.exp(-0.5 * square) / square * (1.0 / math.sqrt(atoms_total * KVECS))
    cw[:, pl.ds(0, kv)] = decay
    cw[:, pl.ds(kv, kv)] = decay

    for one in loads[4:]:
        one.wait()

    @pl.loop(0, half // ROWS)
    def _(i):
        at = pl.ds(pl.multiple_of(i * ROWS, ROWS), ROWS)
        linear = mul(feat[at, :], w_in[...], (1, 0)) + mul(hot[:, at], bias_s[...], (0, 0))
        gate = 0.5 * jnp.tanh(0.5 * linear) + 0.5
        hidden = linear * gate
        slope1[at, :] = gate + hidden * (1.0 - gate)
        hidden = hidden.astype(BF)
        h1[at, :] = hidden
        linear = mul(hidden, w_mid[...], (1, 0))
        gate = 0.5 * jnp.tanh(0.5 * linear) + 0.5
        hidden = linear * gate
        slope2[at, :] = gate + hidden * (1.0 - gate)
        hidden = hidden.astype(BF)
        h2[at, :] = hidden
        ch[x, :, at] = mul(out_t[...], hidden, (1, 1)).astype(BF)

    panels[...] = jnp.zeros_like(panels)

    def phase_tile(base):
        turns[...] = mul(pos_s[:, pl.ds(base, ROWS)], mill_s[...], (0, 0))

        @pl.loop(0, ROWS // STRIP, unroll=4)
        def _(j):
            near = turns[pl.ds(pl.multiple_of(j * STRIP, STRIP), STRIP), :]
            near = near - ((near + TURN_SHIFT) - TURN_SHIFT)
            sq = near * near
            sine = near * (SINE[0] + sq * (SINE[1] + sq * (SINE[2] + sq * SINE[3])))
            cosine = COSINE[0] + sq * (COSINE[1] + sq * (COSINE[2] + sq * (COSINE[3] + sq * COSINE[4])))
            to = pl.ds(pl.multiple_of(base + j * STRIP, STRIP), STRIP)
            phases[to, pl.ds(0, kv)] = (1.0 - sine * sine).astype(BF)
            phases[to, pl.ds(kv, kv)] = (sine * cosine).astype(BF)

    def panel_half(which):
        @pl.loop(0, half // (2 * ROWS))
        def _(i):
            at = pl.ds(pl.multiple_of(i * 2 * ROWS, ROWS), 2 * ROWS)
            base = pl.ds(pl.multiple_of(which * half + i * 2 * ROWS, ROWS), 2 * ROWS)
            panels[...] += mul(ch[which, :, at], phases[base, :], (1, 0))

    def phase_half(which):
        @pl.loop(0, half // ROWS)
        def _(i):
            phase_tile(pl.multiple_of(which * half + i * ROWS, ROWS))

    phase_half(x)
    pl.semaphore_wait(barrier, len(peers))
    charges = copy(ch.at[x], ch.at[x], to_x)
    panel_half(x)
    phase_half(1 - x)
    charges.wait()
    panel_half(1 - x)

    def slab(who):
        return pl.ds(pl.multiple_of(who * width, 128), width)

    sums = []
    for step in range(1, nz):
        pz_s[step] = panels[:, slab(lax.rem(z + step, nz))].astype(BF)
        sums.append(copy(pz_s.at[step], pz_r.at[step], to_z(step)))
    for one in sums:
        one.wait()
    total = panels[:, slab(z)]
    for step in range(1, nz):
        total = total + pz_r[step].astype(F32)
    weighed = total * cw[:, slab(z)]
    w_all[z] = weighed.astype(BF)
    en_mine[...] = jnp.broadcast_to(jnp.sum(total * weighed).reshape(1, 1), en_mine.shape)
    gathers = [copy(w_all.at[z], w_all.at[z], to_z(step)) for step in range(1, nz)]
    shares = [copy(en_mine, en_z.at[step], to_z(step)) for step in range(1, nz)]
    for one in gathers:
        one.wait()

    def potential_half(which, store):
        @pl.loop(0, half // ROWS)
        def _(i):
            at = pl.ds(pl.multiple_of(i * ROWS, ROWS), ROWS)
            base = pl.ds(pl.multiple_of(which * half + i * ROWS, ROWS), ROWS)
            value = mul(w_all[0], phases[base, pl.ds(0, width)], (1, 1))
            for who in range(1, nz):
                value = value + mul(w_all[who], phases[base, pl.ds(who * width, width)], (1, 1))
            store[:, at] = value.astype(store.dtype)

    potential_half(1 - x, pot_s)
    others = copy(pot_s, pot_r, to_x)
    for one in shares:
        one.wait()
    energy = en_mine[...]
    for step in range(1, nz):
        energy = energy + en_z[step]
    en_sum[...] = energy
    energies = copy(en_sum, en_x, to_x)
    potential_half(x, pot)
    energies.wait()
    others.wait()
    energy = (en_sum[...] + en_x[...]) * (1.0 / atoms_total)
    en_o[...] = energy
    scale = (energy[0:1, 0:1] - eref[0]) * (2.0 / atoms_total)
    full = pot[...] + pot_r[...].astype(F32)
    pot[...] = full
    gc[...] = (full * scale).astype(BF)

    @pl.loop(0, half // ROWS)
    def _(i):
        at = pl.ds(pl.multiple_of(i * ROWS, ROWS), ROWS)
        back = mul(gc[:, at], out_t[...], (0, 0))
        g2[at, :] = (back * slope2[at, :]).astype(BF)

    lanes = 128

    def keep(store, first, value):
        for block in range(4):
            store[block, pl.ds(first, value.shape[0]), :] = value[:, block * lanes : (block + 1) * lanes]

    mine = 2 * r + x

    def rep_start(g, out, into):
        out[...] = g[pl.ds(2 * (1 - r), 2)].astype(BF)
        return copy(out, into, to_r)

    def x_start(g, got, out, into):
        out[...] = (g[2 * r + 1 - x] + got[1 - x].astype(F32)).astype(BF)
        return copy(out, into, to_x)

    def z_start(g, got_r, got_x, out, into):
        total = g[mine] + got_r[x].astype(F32) + got_x[...].astype(F32)
        g[mine] = total
        out[...] = total.astype(BF)
        share = out.shape[0] // nz
        made = []
        for step in range(1, nz):
            piece = pl.ds(pl.multiple_of(lax.rem(z + step, nz) * share, 16), share)
            made.append(copy(out.at[piece], into.at[step], to_z(step)))
        return made

    def z_gather(g, got, whole):
        share = got.shape[1]
        piece = pl.ds(pl.multiple_of(z * share, 16), share)
        total = g[mine, piece, :]
        for step in range(1, nz):
            total = total + got[step].astype(F32)
        whole[mine, piece, :] = total.astype(BF)
        return [copy(whole.at[mine, piece], whole.at[mine, piece], to_z(step)) for step in range(1, nz)]

    def finish(made):
        for one in made:
            one.wait()

    def swap_pair(c):
        g, out, into = chunks[c][:3]
        return rep_start(g, out, into)

    def swap_x(c):
        g, _, got, out, into = chunks[c][:5]
        return x_start(g, got, out, into)

    def scatter(c):
        g, _, got_r, _, got_x, out, into, _ = chunks[c]
        return z_start(g, got_r, got_x, out, into)

    def gather(c):
        g, _, _, _, _, _, got, whole = chunks[c]
        return z_gather(g, got, whole)

    def gather_x(c):
        whole = chunks[c][7]
        return copy(whole.at[mine], whole.at[mine], to_x)

    def gather_pair(c):
        whole = chunks[c][7]
        pair = pl.ds(2 * r, 2)
        return copy(whole.at[pair], whole.at[pair], to_r)

    part = h1.shape[1] // 2
    keep(chunks[0][0], 0, mul(h1[:, pl.ds(0, part)], g2[...], (0, 0)))
    pair_0 = swap_pair(0)
    keep(chunks[1][0], 0, mul(h1[:, pl.ds(part, part)], g2[...], (0, 0)))
    pair_1 = swap_pair(1)

    @pl.loop(0, half // ROWS)
    def _(i):
        at = pl.ds(pl.multiple_of(i * ROWS, ROWS), ROWS)
        back = mul(g2[at, :], w_mid[...], (1, 1))
        g1[at, :] = (back * slope1[at, :]).astype(BF)

    pair_0.wait()
    x_0 = swap_x(0)
    pair_1.wait()
    x_1 = swap_x(1)
    features_in = feat.shape[1]
    last = chunks[2][0]
    last[...] = jnp.zeros_like(last)
    keep(last, 0, mul(feat[...], g1[...], (0, 0)))
    keep(last, features_in, mul(gc[...], h2[...], (1, 0)))
    keep(last, features_in + channels, mul(hot[pl.ds(0, 16), :], g1[...], (1, 0)))
    pair_2 = swap_pair(2)
    x_0.wait()
    z_0 = scatter(0)
    pair_2.wait()
    x_2 = swap_x(2)
    x_1.wait()
    z_1 = scatter(1)
    finish(z_0)
    gz_0 = gather(0)
    x_2.wait()
    z_2 = scatter(2)
    finish(z_1)
    gz_1 = gather(1)
    finish(gz_0)
    gx_0 = gather_x(0)
    finish(z_2)
    gz_2 = gather(2)
    finish(gz_1)
    gx_1 = gather_x(1)
    gx_0.wait()
    gr_0 = gather_pair(0)
    finish(gz_2)
    gx_2 = gather_x(2)
    gx_1.wait()
    gr_1 = gather_pair(1)
    gx_2.wait()
    gr_2 = gather_pair(2)
    finish([gr_0, gr_1, gr_2])


def write(features_in, pot, energy, all_0, all_1, all_2, pot_o, en_o, gin_o, gmid_o, gout_o, gbias_o):
    channels = pot.shape[0]
    part = all_0.shape[1]
    en_o[0] = energy[0, 0]
    pot_o[0] = pot[...]
    for block in range(4):
        at = pl.ds(block * 128, 128)
        gmid_o[pl.ds(0, part), at] = all_0[block].astype(F32)
        gmid_o[pl.ds(part, part), at] = all_1[block].astype(F32)
        gin_o[:, at] = all_2[block, pl.ds(0, features_in), :].astype(F32)
        gout_o[:, at] = all_2[block, pl.ds(features_in, channels), :].astype(F32)
        bias_rows = all_2[block, pl.ds(features_in + channels, 16), :].astype(F32)
        gbias_o[:, at] = bias_rows[: gbias_o.shape[0]]


def fits(sizes, args):
    atoms, kv = args[0].shape[2], args[5].shape[1]
    nz = sizes["atoms"]
    return (
        sizes["kvec"] == 2
        and sizes["rep"] == 2
        and nz > 1
        and (2 * kv) % (128 * nz) == 0
        and atoms % (2 * ROWS) == 0
        and args[7].shape[0] % (32 * nz) == 0
        and args[7].shape[1] == 512
        and args[9].shape[0] <= 16
    )


def body(sizes, *args):
    if not fits(sizes, args):
        return plain_body(*args)
    positions, features, _, _, _, miller_index, _, weight_mid, weight_out, species_bias = args
    nz = sizes["atoms"]
    atoms, kv = positions.shape[2], miller_index.shape[1]
    half = atoms // 2
    width = 2 * kv // nz
    inner, channels = weight_out.shape
    features_in = features.shape[2]
    rows_a = inner // 2
    rows_b = -(-(features_in + channels + 16) // (16 * nz)) * 16 * nz

    def vmem(*shape, dtype=F32):
        return pltpu.VMEM(shape, dtype)

    def grads(rows):
        return [
            vmem(4, rows, 128),
            vmem(2, rows, 128, dtype=BF), vmem(2, rows, 128, dtype=BF),
            vmem(rows, 128, dtype=BF), vmem(rows, 128, dtype=BF),
            vmem(rows, 128, dtype=BF), vmem(nz, rows // nz, 128, dtype=BF),
        ]

    scratch = [
        vmem(3, 1, atoms), vmem(half, features_in, dtype=BF), vmem(1, atoms, dtype=jnp.int32),
        vmem(3, kv, dtype=jnp.int32), vmem(features_in, inner, dtype=BF), vmem(inner, inner, dtype=BF),
        vmem(channels, inner, dtype=BF), vmem(*species_bias.shape),
        vmem(16, atoms), vmem(16, atoms, dtype=BF),
        vmem(16, kv), vmem(16, kv, dtype=BF),
        vmem(48, inner), vmem(48, inner, dtype=BF),
        vmem(48, half, dtype=BF), vmem(1, 2 * kv),
        vmem(half, inner, dtype=BF), vmem(half, inner, dtype=BF),
        vmem(half, inner), vmem(half, inner),
        vmem(2, channels, half, dtype=BF), vmem(ROWS, kv), vmem(atoms, 2 * kv, dtype=BF),
        vmem(channels, 2 * kv),
        vmem(nz, channels, width, dtype=BF), vmem(nz, channels, width, dtype=BF),
        vmem(nz, channels, width, dtype=BF),
        vmem(8, 128), vmem(nz, 8, 128), vmem(8, 128), vmem(8, 128),
        vmem(channels, half, dtype=BF), vmem(channels, half, dtype=BF),
        vmem(channels, half, dtype=BF), vmem(half, inner, dtype=BF), vmem(half, inner, dtype=BF),
        *grads(rows_a), *grads(rows_a), *grads(rows_b),
        pltpu.SemaphoreType.DMA((56,)), pltpu.SemaphoreType.DMA((56,)), pltpu.SemaphoreType.DMA((8,)),
    ]
    place = pl.BlockSpec(memory_space=pltpu.VMEM)
    scalar = pl.BlockSpec(memory_space=pltpu.SMEM)
    stay = pl.BlockSpec(memory_space=pltpu.HBM)
    found = pl.pallas_call(
        functools.partial(fused, nz, rows_b),
        out_shape=(
            jax.ShapeDtypeStruct((channels, half), F32),
            jax.ShapeDtypeStruct((8, 128), F32),
            jax.ShapeDtypeStruct((4, rows_a, 128), BF),
            jax.ShapeDtypeStruct((4, rows_a, 128), BF),
            jax.ShapeDtypeStruct((4, rows_b, 128), BF),
        ),
        in_specs=[stay, stay, stay, scalar, scalar] + [stay] * 5,
        out_specs=[place] * 5,
        scratch_shapes=scratch,
        compiler_params=pltpu.CompilerParams(
            collective_id=0, has_side_effects=True, vmem_limit_bytes=60 * 2**20
        ),
    )(jnp.swapaxes(positions, 0, 1), *args[1:8], weight_out.T, species_bias)
    potential, energy, grad_in, grad_mid, grad_out, grad_bias = (
        pl.pallas_call(
            functools.partial(write, features_in),
            out_shape=(
                jax.ShapeDtypeStruct((1, channels, half), F32),
                jax.ShapeDtypeStruct((1,), F32),
                jax.ShapeDtypeStruct((features_in, inner), F32),
                jax.ShapeDtypeStruct((inner, inner), F32),
                jax.ShapeDtypeStruct((channels, inner), F32),
                jax.ShapeDtypeStruct(species_bias.shape, F32),
            ),
            in_specs=[place] * 5,
            out_specs=[place, scalar] + [place] * 4,
            compiler_params=pltpu.CompilerParams(vmem_limit_bytes=60 * 2**20),
        )(*found)
    )
    return (jnp.swapaxes(potential, 1, 2), energy, grad_in, grad_mid, grad_out.T, grad_bias)


def solution(mesh):
    placed = (
        P(("groups", "rep"), None, "atoms"),
        P(("groups", "rep"), "atoms", None),
        P(("groups", "rep"), "atoms"),
        P(("groups", "rep")),
        P(("groups", "rep")),
        P(None, "kvec"),
        P(),
        P(),
        P(),
        P(),
    )
    return jax.shard_map(
        functools.partial(body, dict(mesh.shape)),
        mesh=mesh,
        in_specs=placed,
        out_specs=(
            P(("groups", "rep"), ("atoms", "kvec"), None),
            P(("groups", "rep")),
            P("groups", None),
            P("groups", None),
            P("groups", None),
            P("groups", None),
        ),
        check_vma=False,
    )
```
